32 devices in a mesh: fsdp: 16 (over z, x, core), tp: 2 (over y).
Axes of the slice: x: 2, y: 2, z: 4, core: 2. Of those that a mesh axis runs over, the one named last changes fastest.
Arguments:
- inputs: bfloat16 [32, 736, 1152], P('fsdp', 'tp'), may hold values from -6 to 6
- w_qkv: bfloat16 [3, 1152, 1152], P(None, 'fsdp', 'tp'), may hold values from -0.25 to 0.25
- w_out: bfloat16 [1152, 1152], P('tp', 'fsdp'), may hold values from -0.75 to 0.75
- w_up: bfloat16 [1152, 4304], P('fsdp', 'tp'), may hold values from -0.1875 to 0.1875
- w_down: bfloat16 [4304, 1152], P('tp', 'fsdp'), may hold values from -0.09375 to 0.09375
- norm_gains: float32 [2, 1152], replicated, may hold values from 0.1 to 1.9
- biases: float32 [6, 1152], replicated, may hold values from -3 to 3
- up_bias: float32 [4304], replicated, may hold values from -3 to 3
- cotangent: bfloat16 [32, 736, 1152], P('fsdp', 'tp'), may hold values from -6 to 6
Outputs:
- outputs: bfloat16 [32, 736, 1152], P('fsdp', 'tp')
- input_grad: float32 [32, 736, 1152], P('fsdp', 'tp')
- w_qkv_grad: float32 [3, 1152, 1152], P(None, 'fsdp', 'tp')
- w_out_grad: float32 [1152, 1152], P('tp', 'fsdp')
- w_up_grad: float32 [1152, 4304], P('fsdp', 'tp')
- w_down_grad: float32 [4304, 1152], P('tp', 'fsdp')
- norm_gains_grad: float32 [2, 1152], replicated
- biases_grad: float32 [6, 1152], replicated
- up_bias_grad: float32 [4304], replicated
The draws below stay inside these ranges and needn't reach their ends.
All inputs are finite; a program needn't handle non-finite values.
Results may differ from the reference program's by a relative error of at most 0.018.
The reference program's roundings to bfloat16 on the way count: a program that leaves them out, or rounds other values in their place, can miss the bound.
Values may be sent and summed in bfloat16 or wider, within the bound.
A program may use at most 192 MiB of HBM per device.

```python
import math
import jax
import jax.numpy as jnp
from jax import lax

D = 1152
H = 16
HD = 72
FF = 4304
SEQ = 736
VALID = 729
IMAGES = 32


def level_of(own_key, dims, split, smallest, high):
    gain = 1.0
    for dim, shards_of in split:
        heights = jax.random.uniform(jax.random.fold_in(jax.random.fold_in(own_key, 6), dim), (shards_of,), jnp.float32, smallest / len(split), high / len(split))
        gain = gain * jnp.repeat(jnp.exp(heights), dims[dim] // shards_of).reshape((-1,) + (1,) * (len(dims) - 1 - dim))
    return gain


def bell_draw(rng, dims, scale, bound, cuts=(), dtype=jnp.bfloat16):
    loudness = level_of(rng, dims, cuts, -0.22, 0.18) if cuts else 1.0
    entries = jax.random.normal(rng, dims, jnp.float32) * scale * loudness
    return jnp.minimum(jnp.maximum(entries, -bound), bound).astype(dtype)


def setup_inputs(seed: int = 0) -> dict:
    seeds = jax.random.split(jax.random.key(seed), 10)
    inputs = bell_draw(seeds[0], (IMAGES, SEQ, D), 1.0, 6.0, ((0, 16), (1, 2)))
    w_qkv = bell_draw(seeds[1], (3, D, D), (D // 2) ** -0.5, 0.25, ((1, 16), (2, 2)))
    w_out = bell_draw(seeds[2], (D, D), (D // 16) ** -0.5, 0.75, ((0, 2), (1, 16)))
    w_up = bell_draw(seeds[3], (D, FF), D ** -0.5, 0.1875, ((0, 16), (1, 2)))
    w_down = bell_draw(seeds[4], (FF, D), FF ** -0.5, 0.09375, ((0, 2), (1, 16)))
    norm_gains = jnp.clip(1.0 + 0.18 * jax.random.normal(seeds[5], (2, D), jnp.float32), 0.1, 1.9)
    biases = bell_draw(seeds[6], (6, D), 0.5, 3.0, (), jnp.float32)
    up_bias = bell_draw(seeds[7], (FF,), 0.5, 3.0, (), jnp.float32)
    cotangent = bell_draw(seeds[8], (IMAGES, SEQ, D), 1.0, 6.0, ((0, 16), (1, 2)))
    return dict(inputs=inputs, w_qkv=w_qkv, w_out=w_out, w_up=w_up, w_down=w_down, norm_gains=norm_gains, biases=biases, up_bias=up_bias, cotangent=cotangent)


@jax.custom_vjp
def low(v):
    return lax.optimization_barrier(v.astype(jnp.bfloat16)).astype(jnp.float32)

@jax.custom_vjp
def low_back(v):
    return v

def low_keep(v):
    return (low(v), None)

def low_pass(kept, grad):
    return (grad,)

def back_keep(v):
    return (v, None)

def back_low(kept, grad):
    return (low(grad),)
low.defvjp(low_keep, low_pass)
low_back.defvjp(back_keep, back_low)
norm_eps = 1e-06
gelu_coef = math.sqrt(2.0 / math.pi)
highest = lax.Precision.HIGHEST

def layer_norm(values, scale_row, shift_row):
    average = lax.optimization_barrier(jnp.mean(values, axis=-1, keepdims=True))
    centred = values - average
    spread = lax.optimization_barrier(jnp.mean(centred * centred, axis=-1, keepdims=True))
    return centred * lax.rsqrt(spread + norm_eps) * scale_row + shift_row

def gelu_tanh(pre_act):
    return 0.5 * pre_act * (1.0 + jnp.tanh(gelu_coef * (pre_act + 0.044715 * pre_act * pre_act * pre_act)))

def attend(queries, key_rows, values):
    query_heads = queries.reshape(SEQ, H, HD)
    key_heads = key_rows.reshape(SEQ, H, HD)
    value_heads = values.reshape(SEQ, H, HD)
    scores = jnp.einsum('qhe,khe->hqk', query_heads, key_heads, precision=highest) * (1.0 / math.sqrt(HD))
    scores = low_back(scores)
    visible = jnp.arange(SEQ) < VALID
    scores = jnp.where(visible[None, None, :], scores, -1e+30)
    largest = lax.optimization_barrier(jnp.max(scores, axis=-1, keepdims=True))
    powers = jnp.exp(scores - largest)
    attn_probs = low(powers / lax.optimization_barrier(jnp.sum(powers, axis=-1, keepdims=True)))
    mixed_out = jnp.einsum('hqk,khe->qhe', attn_probs, value_heads, precision=highest)
    return low_back(low(mixed_out.reshape(SEQ, D)))

def forward(residual, w_qkv, w_out, w_up, w_down, norm_gains, biases, up_bias):
    normed_one = low(layer_norm(residual, norm_gains[0], biases[0]))
    queries = low_back(low(jnp.einsum('bsd,de->bse', normed_one, w_qkv[0], precision=highest) + biases[1]))
    key_rows = low_back(low(jnp.einsum('bsd,de->bse', normed_one, w_qkv[1], precision=highest)))
    values = low_back(low(jnp.einsum('bsd,de->bse', normed_one, w_qkv[2], precision=highest) + biases[2]))
    saved_attend = jax.checkpoint(attend)
    mixed_out = lax.map(lambda triple: saved_attend(triple[0], triple[1], triple[2]), (queries, key_rows, values))
    attn_rows = low_back(jnp.einsum('bse,ed->bsd', mixed_out, w_out, precision=highest))
    middle = residual + attn_rows + biases[3]
    normed_two = low(layer_norm(middle, norm_gains[1], biases[4]))
    pre_act = low_back(jnp.einsum('bsd,df->bsf', normed_two, w_up, precision=highest) + up_bias)
    activated = low(gelu_tanh(pre_act))
    mlp_rows = low_back(jnp.einsum('bsf,fd->bsd', activated, w_down, precision=highest))
    return middle + mlp_rows + biases[5]

def reference(inputs, w_qkv, w_out, w_up, w_down, norm_gains, biases, up_bias, cotangent):
    params = (w_qkv.astype(jnp.float32), w_out.astype(jnp.float32), w_up.astype(jnp.float32), w_down.astype(jnp.float32), norm_gains.astype(jnp.float32), biases.astype(jnp.float32), up_bias.astype(jnp.float32))
    per_step = 4
    inputs_all = inputs.astype(jnp.float32).reshape(IMAGES // per_step, per_step, SEQ, D)
    upstream_all = cotangent.astype(jnp.float32).reshape(IMAGES // per_step, per_step, SEQ, D)

    def scan_step(totals, batch_pair):
        output, pull_back = jax.vjp(forward, batch_pair[0], *params)
        gradient_set = pull_back(batch_pair[1])
        summed = tuple((older + newer for older, newer in zip(totals, gradient_set[1:])))
        return (summed, (output, gradient_set[0]))
    zero_set = tuple((jnp.zeros_like(param_now) for param_now in params))
    totals, (output_all, grad_all) = lax.scan(scan_step, zero_set, (inputs_all, upstream_all))
    return (output_all.reshape(IMAGES, SEQ, D).astype(jnp.bfloat16), grad_all.reshape(IMAGES, SEQ, D), totals[0], totals[1], totals[2], totals[3], totals[4], totals[5], totals[6])
```

```python
import math

import jax
import jax.numpy as jnp
from jax import lax
from jax.sharding import PartitionSpec as P

HD = 72
VALID = 729


norm_eps = 1e-06
gelu_coef = math.sqrt(2.0 / math.pi)


def norm_forward(values, scale_row, shift_row):
    average = jnp.mean(values, axis=-1, keepdims=True)
    centred = values - average
    inv_std = lax.rsqrt(jnp.mean(centred * centred, axis=-1, keepdims=True) + norm_eps)
    normed = centred * inv_std
    return (normed * scale_row + shift_row, normed, inv_std)


def norm_backward(upstream, normed, inv_std, scale_row):
    scaled = upstream * scale_row
    back = inv_std * (
        scaled
        - jnp.mean(scaled, axis=-1, keepdims=True)
        - normed * jnp.mean(scaled * normed, axis=-1, keepdims=True)
    )
    return (back, jnp.sum(upstream * normed, axis=0), jnp.sum(upstream, axis=0))


def gelu_tanh(pre_act):
    return (
        0.5
        * pre_act
        * (1.0 + jnp.tanh(gelu_coef * (pre_act + 0.044715 * pre_act * pre_act * pre_act)))
    )


def gelu_slope(pre_act):
    tangent = jnp.tanh(gelu_coef * (pre_act + 0.044715 * pre_act * pre_act * pre_act))
    inner_slope = gelu_coef * (1.0 + 3.0 * 0.044715 * pre_act * pre_act)
    return 0.5 * (1.0 + tangent) + 0.5 * pre_act * (1.0 - tangent * tangent) * inner_slope


def masked_scores(queries, key_rows, positions):
    seq_len = queries.shape[0]
    head_count = queries.shape[1] // HD
    query_heads = queries.reshape(seq_len, head_count, HD)
    key_heads = key_rows.reshape(seq_len, head_count, HD)
    scores = jnp.einsum("qhe,khe->hqk", query_heads, key_heads, preferred_element_type=jnp.float32)
    scores = scores * (1.0 / math.sqrt(HD))
    visible = (positions < VALID)[None, None, :]
    return (jnp.where(visible, scores, -1e30), query_heads, key_heads)


def attend_forward(queries, key_rows, values, positions):
    seq_len = queries.shape[0]
    scores, query_heads, key_heads = masked_scores(queries, key_rows, positions)
    value_heads = values.reshape(seq_len, -1, HD)
    largest = jnp.max(scores, axis=-1, keepdims=True)
    powers = jnp.exp(scores - largest)
    summed = jnp.sum(powers, axis=-1, keepdims=True)
    attn_probs = (powers / summed).astype(jnp.bfloat16)
    mixed_out = jnp.einsum(
        "hqk,khe->qhe", attn_probs, value_heads, preferred_element_type=jnp.float32
    )
    log_totals = (largest + jnp.log(summed))[:, :, 0]
    return (mixed_out.reshape(seq_len, queries.shape[1]).astype(jnp.bfloat16), log_totals)


def attend_backward(queries, key_rows, values, log_totals, d_mixed, positions):
    seq_len = queries.shape[0]
    scores, query_heads, key_heads = masked_scores(queries, key_rows, positions)
    value_heads = values.reshape(seq_len, -1, HD)
    grad_heads = d_mixed.reshape(seq_len, -1, HD)
    probs_full = jnp.exp(scores - log_totals[:, :, None])
    d_probs = jnp.einsum(
        "qhe,khe->hqk", grad_heads, value_heads, preferred_element_type=jnp.float32
    )
    row_inner = jnp.sum(probs_full * d_probs, axis=-1, keepdims=True)
    d_scores = (probs_full * (d_probs - row_inner)).astype(jnp.bfloat16)
    d_values = jnp.einsum(
        "hqk,qhe->khe",
        probs_full.astype(jnp.bfloat16),
        grad_heads,
        preferred_element_type=jnp.float32,
    )
    scale_now = 1.0 / math.sqrt(HD)
    d_queries = (
        jnp.einsum("hqk,khe->qhe", d_scores, key_heads, preferred_element_type=jnp.float32)
        * scale_now
    )
    d_keys = (
        jnp.einsum("hqk,qhe->khe", d_scores, query_heads, preferred_element_type=jnp.float32)
        * scale_now
    )
    parts = [d_queries, d_keys, d_values]
    return jnp.concatenate(
        [part.reshape(seq_len, queries.shape[1]).astype(jnp.bfloat16) for part in parts], axis=1
    )


def dot(left, right, dims):
    return lax.dot_general(left, right, (dims, ((), ())), preferred_element_type=jnp.float32)


ROWS_COLS = ((1,), (0,))
ROWS_ROWS = ((1,), (1,))
COLS_COLS = ((0,), (0,))


def swap_halves(block):
    return lax.ppermute(block, "tp", [(0, 1), (1, 0)])


def gather_rows(block):
    if lax.axis_size("tp") == 2:
        return jnp.concatenate([block, swap_halves(block)], axis=0)
    return lax.all_gather(block, "tp", axis=0, tiled=True)


def scatter_dot(left, right, dims):
    if lax.axis_size("tp") == 2:
        half = left.shape[0] // 2
        away = swap_halves(dot(left[half:], right, dims).astype(jnp.bfloat16))
        return dot(left[:half], right, dims) + away.astype(jnp.float32)
    return lax.psum_scatter(
        dot(left, right, dims).astype(jnp.bfloat16), "tp", scatter_dimension=0, tiled=True
    ).astype(jnp.float32)


def gather_weight(shard):
    return lax.all_gather(shard, "fsdp", axis=0, tiled=True)


def scatter_weight(whole):
    return lax.psum_scatter(
        whole.astype(jnp.bfloat16), "fsdp", scatter_dimension=0, tiled=True
    ).astype(jnp.float32)


def per_device(inputs, w_qkv, w_out, w_up, w_down, norm_gains, biases, up_bias, cotangent):
    image_count, rows_here, width = inputs.shape
    images = range(image_count)
    local_cols = w_qkv.shape[2]
    unit_count = w_up.shape[1]
    shard_rows = w_qkv.shape[1]
    tp_index = lax.axis_index("tp")
    seq_len = rows_here * lax.axis_size("tp")
    col_start = tp_index * local_cols
    unit_start = tp_index * unit_count
    positions = lax.iota(jnp.int32, seq_len)
    if lax.axis_size("tp") == 2:
        positions = positions + tp_index * rows_here
        positions = jnp.where(positions >= seq_len, positions - seq_len, positions)

    qkv_all = gather_weight(w_qkv.transpose(1, 0, 2).reshape(shard_rows, 3 * local_cols))
    out_all = gather_weight(w_out.T)
    up_all = gather_weight(w_up)
    down_all = gather_weight(w_down.T)
    query_bias = lax.dynamic_slice_in_dim(biases[1], col_start, local_cols)
    value_bias = lax.dynamic_slice_in_dim(biases[2], col_start, local_cols)
    unit_bias = lax.dynamic_slice_in_dim(up_bias, unit_start, unit_count)
    qkv_bias = jnp.concatenate([query_bias, jnp.zeros_like(query_bias), value_bias])

    residual = [inputs[i].astype(jnp.float32) for i in images]
    first = [norm_forward(residual[i], norm_gains[0], biases[0]) for i in images]
    gathered_one = [gather_rows(first[i][0].astype(jnp.bfloat16)) for i in images]
    grad_rows = [gather_rows(cotangent[i]) for i in images]

    saved, mixed, middle, second, gathered_two = [], [], [], [], []
    for i in images:
        projected = (dot(gathered_one[i], qkv_all, ROWS_COLS) + qkv_bias).astype(jnp.bfloat16)
        queries, key_rows, values = (
            projected[:, c * local_cols : (c + 1) * local_cols] for c in range(3)
        )
        mixed_out, log_totals = attend_forward(queries, key_rows, values, positions)
        saved.append((queries, key_rows, values, log_totals))
        mixed.append(mixed_out)
        middle.append(residual[i] + scatter_dot(mixed_out, out_all, ROWS_ROWS) + biases[3])
        second.append(norm_forward(middle[i], norm_gains[1], biases[4]))
        gathered_two.append(gather_rows(second[i][0].astype(jnp.bfloat16)))

    activated, d_pre, outputs, d_normed_two = [], [], [], []
    for i in images:
        pre_act = dot(gathered_two[i], up_all, ROWS_COLS) + unit_bias
        activated.append(gelu_tanh(pre_act).astype(jnp.bfloat16))
        d_act = dot(grad_rows[i], down_all, ROWS_COLS)
        d_pre.append((d_act * gelu_slope(pre_act)).astype(jnp.bfloat16))
        d_normed_two.append(scatter_dot(d_pre[i], up_all, ROWS_ROWS))
        mlp_rows = scatter_dot(activated[i], down_all, ROWS_ROWS)
        outputs.append((middle[i] + mlp_rows + biases[5]).astype(jnp.bfloat16))

    def joined(parts):
        return jnp.concatenate(parts, axis=0)

    grads_whole, units_whole = joined(grad_rows), joined(d_pre)
    down_grad = scatter_weight(dot(grads_whole, joined(activated), COLS_COLS)).T
    up_grad = scatter_weight(dot(joined(gathered_two), units_whole, COLS_COLS))
    unit_sums = jnp.sum(units_whole, axis=0, dtype=jnp.float32)

    gain_two, shift_two, d_middle, branch = [], [], [], []
    for i in images:
        back, gain_part, shift_part = norm_backward(
            d_normed_two[i], second[i][1], second[i][2], norm_gains[1]
        )
        gain_two.append(gain_part)
        shift_two.append(shift_part)
        d_middle.append(cotangent[i].astype(jnp.float32) + back)
        branch.append(gather_rows(d_middle[i].astype(jnp.bfloat16)))

    d_qkv, d_normed_one = [], []
    for i in images:
        d_mixed = dot(branch[i], out_all, ROWS_COLS).astype(jnp.bfloat16)
        d_qkv.append(attend_backward(*saved[i], d_mixed, positions))
        d_normed_one.append(scatter_dot(d_qkv[i], qkv_all, ROWS_ROWS))
    out_grad = scatter_weight(dot(joined(branch), joined(mixed), COLS_COLS)).T
    qkv_whole = joined(d_qkv)
    qkv_grad = scatter_weight(dot(joined(gathered_one), qkv_whole, COLS_COLS))
    qkv_grad = qkv_grad.reshape(shard_rows, 3, local_cols).transpose(1, 0, 2)
    qkv_sums = jnp.sum(qkv_whole, axis=0, dtype=jnp.float32)

    input_grad, gain_one, shift_one = [], [], []
    for i in images:
        back, gain_part, shift_part = norm_backward(
            d_normed_one[i], first[i][1], first[i][2], norm_gains[0]
        )
        gain_one.append(gain_part)
        shift_one.append(shift_part)
        input_grad.append(d_middle[i] + back)

    blank_row = jnp.zeros((width,), jnp.float32)
    query_sums = lax.dynamic_update_slice_in_dim(blank_row, qkv_sums[:local_cols], col_start, 0)
    value_sums = lax.dynamic_update_slice_in_dim(blank_row, qkv_sums[2 * local_cols :], col_start, 0)
    unit_row = lax.dynamic_update_slice_in_dim(jnp.zeros_like(up_bias), unit_sums, unit_start, 0)
    out_sums = sum(jnp.sum(d_middle[i], axis=0) for i in images)
    top_sums = jnp.sum(cotangent, axis=(0, 1), dtype=jnp.float32)
    pieces = [
        sum(gain_one), sum(shift_one), query_sums, value_sums,
        sum(gain_two), sum(shift_two), out_sums, top_sums, unit_row,
    ]
    total = lax.psum(jnp.concatenate(pieces), ("fsdp", "tp"))
    rows = total[: 8 * width].reshape(8, width)
    gain_total = jnp.stack([rows[0], rows[4]])
    bias_total = jnp.stack([rows[1], rows[2], rows[3], rows[6], rows[5], rows[7]])
    return (
        jnp.stack(outputs),
        jnp.stack(input_grad),
        qkv_grad,
        out_grad,
        up_grad,
        down_grad,
        gain_total,
        bias_total,
        total[8 * width :],
    )


def solution(mesh):
    return jax.shard_map(
        per_device,
        mesh=mesh,
        in_specs=(
            P("fsdp", "tp", None),
            P(None, "fsdp", "tp"),
            P("tp", "fsdp"),
            P("fsdp", "tp"),
            P("tp", "fsdp"),
            P(),
            P(),
            P(),
            P("fsdp", "tp", None),
        ),
        out_specs=(
            P("fsdp", "tp", None),
            P("fsdp", "tp", None),
            P(None, "fsdp", "tp"),
            P("tp", "fsdp"),
            P("fsdp", "tp"),
            P("tp", "fsdp"),
            P(),
            P(),
            P(),
        ),
        check_vma=False,
    )
```

```python
import math

import jax
import jax.numpy as jnp
from jax import lax
from jax.sharding import PartitionSpec as P

HD = 72
VALID = 729


norm_eps = 1e-06
gelu_coef = math.sqrt(2.0 / math.pi)


def norm_forward(values, scale_row, shift_row):
    average = jnp.mean(values, axis=-1, keepdims=True)
    centred = values - average
    inv_std = lax.rsqrt(jnp.mean(centred * centred, axis=-1, keepdims=True) + norm_eps)
    normed = centred * inv_std
    return (normed * scale_row + shift_row, normed, inv_std)


def norm_backward(upstream, normed, inv_std, scale_row):
    scaled = upstream * scale_row
    back = inv_std * (
        scaled
        - jnp.mean(scaled, axis=-1, keepdims=True)
        - normed * jnp.mean(scaled * normed, axis=-1, keepdims=True)
    )
    return (back, jnp.sum(upstream * normed, axis=0), jnp.sum(upstream, axis=0))


def gelu_tanh(pre_act):
    return (
        0.5
        * pre_act
        * (1.0 + jnp.tanh(gelu_coef * (pre_act + 0.044715 * pre_act * pre_act * pre_act)))
    )


def gelu_slope(pre_act):
    tangent = jnp.tanh(gelu_coef * (pre_act + 0.044715 * pre_act * pre_act * pre_act))
    inner_slope = gelu_coef * (1.0 + 3.0 * 0.044715 * pre_act * pre_act)
    return 0.5 * (1.0 + tangent) + 0.5 * pre_act * (1.0 - tangent * tangent) * inner_slope


def masked_scores(queries, key_rows, positions):
    seq_len = queries.shape[0]
    head_count = queries.shape[1] // HD
    query_heads = queries.reshape(seq_len, head_count, HD)
    key_heads = key_rows.reshape(seq_len, head_count, HD)
    scores = jnp.einsum("qhe,khe->hqk", query_heads, key_heads, preferred_element_type=jnp.float32)
    scores = scores * (1.0 / math.sqrt(HD))
    visible = (positions < VALID)[None, None, :]
    return (jnp.where(visible, scores, -1e30), query_heads, key_heads)


def attend_forward(queries, key_rows, values, positions):
    seq_len = queries.shape[0]
    scores, query_heads, key_heads = masked_scores(queries, key_rows, positions)
    value_heads = values.reshape(seq_len, -1, HD)
    largest = jnp.max(scores, axis=-1, keepdims=True)
    powers = jnp.exp(scores - largest)
    summed = jnp.sum(powers, axis=-1, keepdims=True)
    attn_probs = (powers / summed).astype(jnp.bfloat16)
    mixed_out = jnp.einsum(
        "hqk,khe->qhe", attn_probs, value_heads, preferred_element_type=jnp.float32
    )
    log_totals = (largest + jnp.log(summed))[:, :, 0]
    return (mixed_out.reshape(seq_len, queries.shape[1]).astype(jnp.bfloat16), log_totals)


def attend_backward(queries, key_rows, values, log_totals, d_mixed, positions):
    seq_len = queries.shape[0]
    scores, query_heads, key_heads = masked_scores(queries, key_rows, positions)
    value_heads = values.reshape(seq_len, -1, HD)
    grad_heads = d_mixed.reshape(seq_len, -1, HD)
    probs_full = jnp.exp(scores - log_totals[:, :, None])
    d_probs = jnp.einsum(
        "qhe,khe->hqk", grad_heads, value_heads, preferred_element_type=jnp.float32
    )
    row_inner = jnp.sum(probs_full * d_probs, axis=-1, keepdims=True)
    d_scores = (probs_full * (d_probs - row_inner)).astype(jnp.bfloat16)
    d_values = jnp.einsum(
        "hqk,qhe->khe",
        probs_full.astype(jnp.bfloat16),
        grad_heads,
        preferred_element_type=jnp.float32,
    )
    scale_now = 1.0 / math.sqrt(HD)
    d_queries = (
        jnp.einsum("hqk,khe->qhe", d_scores, key_heads, preferred_element_type=jnp.float32)
        * scale_now
    )
    d_keys = (
        jnp.einsum("hqk,qhe->khe", d_scores, query_heads, preferred_element_type=jnp.float32)
        * scale_now
    )
    parts = [d_queries, d_keys, d_values]
    return jnp.concatenate(
        [part.reshape(seq_len, queries.shape[1]).astype(jnp.bfloat16) for part in parts], axis=1
    )


def dot(left, right, dims):
    return lax.dot_general(left, right, (dims, ((), ())), preferred_element_type=jnp.float32)


ROWS_COLS = ((1,), (0,))
ROWS_ROWS = ((1,), (1,))
COLS_COLS = ((0,), (0,))


def swap_halves(block):
    return lax.ppermute(block, "tp", [(0, 1), (1, 0)])


def gather_rows(block):
    if lax.axis_size("tp") == 2:
        return jnp.concatenate([block, swap_halves(block)], axis=0)
    return lax.all_gather(block, "tp", axis=0, tiled=True)


def scatter_dot(left, right, dims):
    if lax.axis_size("tp") == 2:
        half = left.shape[0] // 2
        away = swap_halves(dot(left[half:], right, dims).astype(jnp.bfloat16))
        return dot(left[:half], right, dims) + away.astype(jnp.float32)
    return lax.psum_scatter(
        dot(left, right, dims).astype(jnp.bfloat16), "tp", scatter_dimension=0, tiled=True
    ).astype(jnp.float32)


def gather_weight(shard):
    return lax.all_gather(shard, "fsdp", axis=0, tiled=True)


def scatter_weight(whole):
    return lax.psum_scatter(
        whole.astype(jnp.bfloat16), "fsdp", scatter_dimension=0, tiled=False
    ).astype(jnp.float32)


def by_shard(whole):
    return whole.astype(jnp.bfloat16).reshape(lax.axis_size("fsdp"), -1, whole.shape[1])


def per_device(inputs, w_qkv, w_out, w_up, w_down, norm_gains, biases, up_bias, cotangent):
    image_count, rows_here, width = inputs.shape
    images = range(image_count)
    local_cols = w_qkv.shape[2]
    unit_count = w_up.shape[1]
    shard_rows = w_qkv.shape[1]
    tp_index = lax.axis_index("tp")
    seq_len = rows_here * lax.axis_size("tp")
    col_start = tp_index * local_cols
    unit_start = tp_index * unit_count
    positions = lax.iota(jnp.int32, seq_len)
    if lax.axis_size("tp") == 2:
        positions = positions + tp_index * rows_here
        positions = jnp.where(positions >= seq_len, positions - seq_len, positions)

    qkv_all = gather_weight(w_qkv.transpose(1, 0, 2).reshape(shard_rows, 3 * local_cols))
    out_all = gather_weight(w_out.T)
    up_all = gather_weight(w_up)
    down_all = gather_weight(w_down.T)
    query_bias = lax.dynamic_slice_in_dim(biases[1], col_start, local_cols)
    value_bias = lax.dynamic_slice_in_dim(biases[2], col_start, local_cols)
    unit_bias = lax.dynamic_slice_in_dim(up_bias, unit_start, unit_count)
    qkv_bias = jnp.concatenate([query_bias, jnp.zeros_like(query_bias), value_bias])

    residual = [inputs[i].astype(jnp.float32) for i in images]
    first = [norm_forward(residual[i], norm_gains[0], biases[0]) for i in images]
    gathered_one = [gather_rows(first[i][0].astype(jnp.bfloat16)) for i in images]
    grad_rows = [gather_rows(cotangent[i]) for i in images]

    saved, mixed, middle, second, gathered_two = [], [], [], [], []
    for i in images:
        projected = (dot(gathered_one[i], qkv_all, ROWS_COLS) + qkv_bias).astype(jnp.bfloat16)
        queries, key_rows, values = (
            projected[:, c * local_cols : (c + 1) * local_cols] for c in range(3)
        )
        mixed_out, log_totals = attend_forward(queries, key_rows, values, positions)
        saved.append((queries, key_rows, values, log_totals))
        mixed.append(mixed_out)
        middle.append(residual[i] + scatter_dot(mixed_out, out_all, ROWS_ROWS) + biases[3])
        second.append(norm_forward(middle[i], norm_gains[1], biases[4]))
        gathered_two.append(gather_rows(second[i][0].astype(jnp.bfloat16)))

    activated, d_pre, outputs, d_normed_two = [], [], [], []
    for i in images:
        pre_act = dot(gathered_two[i], up_all, ROWS_COLS) + unit_bias
        activated.append(gelu_tanh(pre_act).astype(jnp.bfloat16))
        d_act = dot(grad_rows[i], down_all, ROWS_COLS)
        d_pre.append((d_act * gelu_slope(pre_act)).astype(jnp.bfloat16))
        d_normed_two.append(scatter_dot(d_pre[i], up_all, ROWS_ROWS))
        mlp_rows = scatter_dot(activated[i], down_all, ROWS_ROWS)
        outputs.append((middle[i] + mlp_rows + biases[5]).astype(jnp.bfloat16))

    def joined(parts):
        return jnp.concatenate(parts, axis=0)

    grads_whole, units_whole = joined(grad_rows), joined(d_pre)
    down_whole = by_shard(dot(grads_whole, joined(activated), COLS_COLS))
    up_whole = by_shard(dot(joined(gathered_two), units_whole, COLS_COLS))
    down_whole, up_whole, d_normed_two = lax.optimization_barrier(
        (down_whole, up_whole, d_normed_two)
    )
    down_grad = scatter_weight(down_whole).T
    up_grad = scatter_weight(up_whole)
    unit_sums = jnp.sum(units_whole, axis=0, dtype=jnp.float32)

    gain_two, shift_two, d_middle, branch = [], [], [], []
    for i in images:
        back, gain_part, shift_part = norm_backward(
            d_normed_two[i], second[i][1], second[i][2], norm_gains[1]
        )
        gain_two.append(gain_part)
        shift_two.append(shift_part)
        d_middle.append(cotangent[i].astype(jnp.float32) + back)
        branch.append(gather_rows(d_middle[i].astype(jnp.bfloat16)))

    d_qkv, d_normed_one = [], []
    for i in images:
        d_mixed = dot(branch[i], out_all, ROWS_COLS).astype(jnp.bfloat16)
        d_qkv.append(attend_backward(*saved[i], d_mixed, positions))
        d_normed_one.append(scatter_dot(d_qkv[i], qkv_all, ROWS_ROWS))
    out_grad = scatter_weight(by_shard(dot(joined(branch), joined(mixed), COLS_COLS))).T
    qkv_whole = joined(d_qkv)
    qkv_grad = scatter_weight(by_shard(dot(joined(gathered_one), qkv_whole, COLS_COLS)))
    qkv_grad = qkv_grad.reshape(shard_rows, 3, local_cols).transpose(1, 0, 2)
    qkv_sums = jnp.sum(qkv_whole, axis=0, dtype=jnp.float32)

    input_grad, gain_one, shift_one = [], [], []
    for i in images:
        back, gain_part, shift_part = norm_backward(
            d_normed_one[i], first[i][1], first[i][2], norm_gains[0]
        )
        gain_one.append(gain_part)
        shift_one.append(shift_part)
        input_grad.append(d_middle[i] + back)

    blank_row = jnp.zeros((width,), jnp.float32)
    query_sums = lax.dynamic_update_slice_in_dim(blank_row, qkv_sums[:local_cols], col_start, 0)
    value_sums = lax.dynamic_update_slice_in_dim(blank_row, qkv_sums[2 * local_cols :], col_start, 0)
    unit_row = lax.dynamic_update_slice_in_dim(jnp.zeros_like(up_bias), unit_sums, unit_start, 0)
    out_sums = sum(jnp.sum(d_middle[i], axis=0) for i in images)
    top_sums = jnp.sum(cotangent, axis=(0, 1), dtype=jnp.float32)
    pieces = [
        sum(gain_one), sum(shift_one), query_sums, value_sums,
        sum(gain_two), sum(shift_two), out_sums, top_sums, unit_row,
    ]
    total = lax.psum(jnp.concatenate(pieces), ("fsdp", "tp"))
    rows = total[: 8 * width].reshape(8, width)
    gain_total = jnp.stack([rows[0], rows[4]])
    bias_total = jnp.stack([rows[1], rows[2], rows[3], rows[6], rows[5], rows[7]])
    return (
        jnp.stack(outputs),
        jnp.stack(input_grad),
        qkv_grad,
        out_grad,
        up_grad,
        down_grad,
        gain_total,
        bias_total,
        total[8 * width :],
    )


def solution(mesh):
    return jax.shard_map(
        per_device,
        mesh=mesh,
        in_specs=(
            P("fsdp", "tp", None),
            P(None, "fsdp", "tp"),
            P("tp", "fsdp"),
            P("fsdp", "tp"),
            P("tp", "fsdp"),
            P(),
            P(),
            P(),
            P("fsdp", "tp", None),
        ),
        out_specs=(
            P("fsdp", "tp", None),
            P("fsdp", "tp", None),
            P(None, "fsdp", "tp"),
            P("tp", "fsdp"),
            P("fsdp", "tp"),
            P("tp", "fsdp"),
            P(),
            P(),
            P(),
        ),
        check_vma=False,
    )
```
